256 devices in a mesh: dp: 32 (over z, x), fsdp: 8 (over y, core).
Axes of the slice: x: 4, y: 4, z: 8, core: 2. Of those that a mesh axis runs over, the one named last changes fastest.
Arguments:
- incoming_feature_maps: bfloat16 [256, 8, 8, 3072], P('dp', None, None, 'fsdp'), may hold values from -6 to 6
- spatial_filter_tensor: bfloat16 [7, 7, 3072], P(None, None, 'fsdp'), may hold values from -0.875 to 0.875
- spatial_filter_offset: float32 [3072], P('fsdp'), may hold values from -3 to 3
- unit_layernorm_multiplier: float32 [3072], replicated, may hold values from 0.5 to 1.5
- unit_layernorm_offset_vector: float32 [3072], replicated, may hold values from -3 to 3
- expansion_linear_map: bfloat16 [3072, 12288], P('dp', 'fsdp'), may hold values from -0.109375 to 0.109375
- expansion_offset: float32 [12288], P('fsdp'), may hold values from -3 to 3
- contraction_linear_map: bfloat16 [12288, 3072], P('fsdp', 'dp'), may hold values from -0.109375 to 0.109375
- contraction_offset: float32 [3072], P('fsdp'), may hold values from -3 to 3
- residual_channel_factor: float32 [3072], P('fsdp'), may hold values from 0.3 to 1.5
- readout_layernorm_multiplier: float32 [3072], P('fsdp'), may hold values from 0.5 to 1.5
- readout_layernorm_offset: float32 [3072], P('fsdp'), may hold values from -3 to 3
- readout_linear_map: bfloat16 [3072, 768], P('fsdp'), may hold values from -0.109375 to 0.109375
- learner_caption_vectors: bfloat16 [16384, 768], P(('dp', 'fsdp')), may hold values from -6 to 6
- mentor_caption_vectors: bfloat16 [16384, 768], P(('dp', 'fsdp')), may hold values from -6 to 6
- mentor_picture_vectors: bfloat16 [256, 768], P('dp'), may hold values from -6 to 6
- divisor_per_slot: float32 [64], replicated, may hold values from 0.003 to 0.07
- active_program_slot: int32 [1], replicated, may hold values from 0 to 63
- matching_caption_slot: int32 [256], replicated, may hold values from 0 to 16383
Outputs:
- block_out: bfloat16 [256, 8, 8, 3072], P('dp', None, None, 'fsdp')
- embedding: float32 [256, 768], P('dp')
- losses: float32 [256], P(('dp', 'fsdp'))
The draws below stay inside these ranges and needn't reach their ends.
All inputs are finite; a program needn't handle non-finite values.
Results may differ from the reference program's by a relative error of at most 0.015.
Values may be sent and summed in bfloat16 or wider, within the bound.
No kernel may reach another device: no remote copies, remote signals or barrier semaphores. Data moves between devices by JAX's collectives and lax.ppermute only.
A program may use at most 128 MiB of HBM per device.

```python
import math
import jax
import jax.numpy as jnp
from jax import lax

D = 3072
FF = 12288
E = 768
SIDE = 8
KERNEL = 7
STEPS = 64
IMAGES = 256
BATCH = 16384
N_DP = 32
N_FSDP = 8


def shared_keys(key):
    return jax.random.normal(key, (BATCH, E), jnp.float32)


def draw_mentor_caption_vectors(key, part):
    base = shared_keys(key)
    return jnp.clip(base, -6.0, 6.0).astype(jnp.bfloat16)


def draw_mentor_picture_vectors(key, part):
    key = jax.random.fold_in(key, 12)
    own = jax.random.normal(key, (IMAGES, E), jnp.float32)
    return jnp.clip(own, -6.0, 6.0).astype(jnp.bfloat16)


def draw_divisor_per_slot(key, part):
    key = jax.random.fold_in(key, 13)
    lowest = 0.01
    highest = 0.07
    fraction = jax.random.uniform(key, (STEPS,), jnp.float32)
    return jnp.exp(jnp.log(lowest) + fraction * (jnp.log(highest) - jnp.log(lowest)))


def set_ends(values, key, low, high):
    place = [jax.random.randint(jax.random.fold_in(key, axis), (), 0, length) for axis, length in enumerate(values.shape)]
    widest = values.shape.index(max(values.shape))
    neighbour = place[:widest] + [(place[widest] + 1) % values.shape[widest]] + place[widest + 1:]
    return values.at[tuple(place)].set(low).at[tuple(neighbour)].set(high)


def strengthened(values, own_key, source, target, shards_of, factor):
    def block_of(dim):
        return (jnp.arange(values.shape[dim]) // (values.shape[dim] // shards_of)).reshape((-1,) + (1,) * (values.ndim - 1 - dim))

    near = jax.random.permutation(own_key, shards_of)[block_of(target)]
    other_side = (block_of(target) + shards_of // 2) % shards_of
    return jnp.where((block_of(source) == near) | (block_of(source) == other_side), factor * values, values)


def steps_of(rng, shape, pieces, least, high):
    level = 1.0
    for dim, blocks in pieces:
        draws = jax.random.uniform(jax.random.fold_in(jax.random.fold_in(rng, 6), dim), (blocks,), jnp.float32, least / len(pieces), high / len(pieces))
        level = level * jnp.repeat(jnp.exp(draws), shape[dim] // blocks).reshape((-1,) + (1,) * (len(shape) - 1 - dim))
    return level


def scatter_about(key, dims, scale, most, shards=(), kind=jnp.bfloat16):
    level = steps_of(key, dims, shards, -0.22, 0.18) if shards else 1.0
    values = jax.random.normal(key, dims, jnp.float32) * scale * level
    return jnp.minimum(jnp.maximum(values, -most), most).astype(kind)


def bell_draw_with(own_key, extent, scale, bound, shards, heavy, dtype=jnp.bfloat16):
    array = scale * jax.random.normal(own_key, extent, jnp.float32)
    if shards:
        array = array * steps_of(own_key, extent, shards, -0.22, 0.18)
    return jnp.clip(strengthened(array, jax.random.fold_in(own_key, 3), *heavy), -bound, bound).astype(dtype)


def setup_inputs(seed: int = 0) -> dict:
    seeds = jax.random.split(jax.random.key(seed), 20)
    incoming_feature_maps = scatter_about(seeds[0], (IMAGES, SIDE, SIDE, D), 1.0, 6.0, ((0, 32), (3, 8)))
    spatial_filter_tensor = scatter_about(seeds[1], (KERNEL, KERNEL, D), (KERNEL * KERNEL) ** -0.5, 0.875, ((2, 8),))
    spatial_filter_offset = scatter_about(seeds[2], (D,), 0.5, 3.0, ((0, 8),), jnp.float32)
    unit_layernorm_multiplier = jnp.clip(jax.random.uniform(seeds[3], (D,), jnp.float32, 0.5, 1.5), 0.5, 1.5)
    unit_layernorm_offset_vector = scatter_about(seeds[4], (D,), 0.5, 3.0, (), jnp.float32)
    expansion_linear_map = scatter_about(seeds[5], (D, FF), D ** -0.5, 0.109375, ((0, 32), (1, 8)))
    expansion_offset = scatter_about(seeds[6], (FF,), 0.5, 3.0, ((0, 8),), jnp.float32)
    contraction_linear_map = bell_draw_with(seeds[7], (FF, D), FF ** -0.5, 0.109375, ((0, 8), (1, 32)), (0, 1, 32, 2.75))
    contraction_offset = scatter_about(seeds[8], (D,), 0.5, 3.0, ((0, 8),), jnp.float32)
    residual_channel_factor = jnp.clip(jnp.exp(math.log(1.5) - 1.60943787 * jax.random.uniform(seeds[9], (D,), jnp.float32) ** steps_of(seeds[9], (D,), ((0, 8),), -0.2, 0.2)), 0.3, 1.5)
    readout_layernorm_multiplier = jnp.clip(0.5 + 1.0 * jax.random.uniform(seeds[10], (D,), jnp.float32) ** steps_of(seeds[10], (D,), ((0, 8),), -0.2, 0.2), 0.5, 1.5)
    readout_layernorm_offset = scatter_about(seeds[11], (D,), 0.5, 3.0, ((0, 8),), jnp.float32)
    readout_linear_map = scatter_about(seeds[12], (D, E), D ** -0.5, 0.109375, ((0, 8),))
    learner_caption_vectors = scatter_about(seeds[13], (BATCH, E), 1.0, 6.0, ((0, 256),))
    mentor_caption_vectors = draw_mentor_caption_vectors(jax.random.fold_in(seeds[19], 71), 0)
    mentor_picture_vectors = draw_mentor_picture_vectors(jax.random.fold_in(seeds[19], 71), 0)
    divisor_per_slot = draw_divisor_per_slot(jax.random.fold_in(seeds[19], 71), 0)
    active_program_slot = jax.random.randint(seeds[17], (1,), 0, STEPS).astype(jnp.int32)
    matching_caption_slot = set_ends(jax.random.randint(seeds[18], (IMAGES,), 0, BATCH), jax.random.fold_in(seeds[18], 1), 0, BATCH - 1).astype(jnp.int32)
    return {"incoming_feature_maps": incoming_feature_maps, "spatial_filter_tensor": spatial_filter_tensor, "spatial_filter_offset": spatial_filter_offset, "unit_layernorm_multiplier": unit_layernorm_multiplier, "unit_layernorm_offset_vector": unit_layernorm_offset_vector, "expansion_linear_map": expansion_linear_map, "expansion_offset": expansion_offset, "contraction_linear_map": contraction_linear_map, "contraction_offset": contraction_offset, "residual_channel_factor": residual_channel_factor, "readout_layernorm_multiplier": readout_layernorm_multiplier, "readout_layernorm_offset": readout_layernorm_offset, "readout_linear_map": readout_linear_map, "learner_caption_vectors": learner_caption_vectors, "mentor_caption_vectors": mentor_caption_vectors, "mentor_picture_vectors": mentor_picture_vectors, "divisor_per_slot": divisor_per_slot, "active_program_slot": active_program_slot, "matching_caption_slot": matching_caption_slot}


EPSILON = 1e-06
HIGHEST = lax.Precision.HIGHEST

def depthwise(incoming_feature_maps, spatial_filter_tensor, spatial_filter_offset):
    radius = KERNEL // 2
    padded = jnp.pad(incoming_feature_maps.astype(jnp.float32), ((0, 0), (radius, radius), (radius, radius), (0, 0)))
    summed = jnp.zeros(incoming_feature_maps.shape, jnp.float32)
    for vertical in range(KERNEL):
        for horizontal in range(KERNEL):
            window = padded[:, vertical:vertical + SIDE, horizontal:horizontal + SIDE, :]
            summed = summed + spatial_filter_tensor[vertical, horizontal].astype(jnp.float32) * window
    return (summed + spatial_filter_offset).astype(jnp.bfloat16)

def layer_norm(values, gain, shift):
    mean_val = lax.optimization_barrier(jnp.mean(values, -1, keepdims=True))
    centered = values - mean_val
    spread = lax.optimization_barrier(jnp.mean(centered * centered, -1, keepdims=True))
    return centered / jnp.sqrt(spread + EPSILON) * gain + shift

def unit_rows(values):
    return (values / jnp.sqrt(lax.optimization_barrier(jnp.sum(values * values, -1, keepdims=True)) + EPSILON)).astype(jnp.bfloat16)

def log_total(scores):
    top_score = lax.optimization_barrier(jnp.max(scores, 1, keepdims=True))
    return top_score[:, 0] + jnp.log(lax.optimization_barrier(jnp.sum(jnp.exp(scores - top_score), 1)))

def reference(incoming_feature_maps, spatial_filter_tensor, spatial_filter_offset, unit_layernorm_multiplier, unit_layernorm_offset_vector, expansion_linear_map, expansion_offset, contraction_linear_map, contraction_offset, residual_channel_factor, readout_layernorm_multiplier, readout_layernorm_offset, readout_linear_map, learner_caption_vectors, mentor_caption_vectors, mentor_picture_vectors, divisor_per_slot, active_program_slot, matching_caption_slot):
    convolved = depthwise(incoming_feature_maps, spatial_filter_tensor, spatial_filter_offset)
    normed = layer_norm(convolved.astype(jnp.float32), unit_layernorm_multiplier, unit_layernorm_offset_vector).astype(jnp.bfloat16)
    group_rows = IMAGES * SIDE * SIDE // N_DP
    blocks = normed.reshape(N_DP, group_rows, D)
    part_width = FF // N_FSDP

    def mlp_block(token_block):
        preact = jnp.dot(token_block, expansion_linear_map, preferred_element_type=jnp.float32) + expansion_offset
        hidden = jax.nn.gelu(preact, approximate=False).astype(jnp.bfloat16)
        branch = jnp.zeros((group_rows, D), jnp.float32)
        for member in range(N_FSDP):
            partial_value = jnp.dot(hidden[:, member * part_width:(member + 1) * part_width], contraction_linear_map[member * part_width:(member + 1) * part_width], preferred_element_type=jnp.float32)
            branch = branch + lax.optimization_barrier(partial_value.astype(jnp.bfloat16)).astype(jnp.float32)
        return branch
    branch = lax.map(mlp_block, blocks).reshape(incoming_feature_maps.shape)
    block_out = (incoming_feature_maps.astype(jnp.float32) + residual_channel_factor * (branch + contraction_offset)).astype(jnp.bfloat16)
    pooled = lax.optimization_barrier(jnp.mean(block_out.astype(jnp.float32), axis=(1, 2)))
    head_normed = layer_norm(pooled, readout_layernorm_multiplier, readout_layernorm_offset)
    embedding = jnp.dot(head_normed, readout_linear_map.astype(jnp.float32), precision=HIGHEST)
    logit_divisor = lax.dynamic_index_in_dim(divisor_per_slot, active_program_slot[0], keepdims=False)
    learner_vector_list = unit_rows(embedding)
    mentor_vector_list = unit_rows(mentor_picture_vectors.astype(jnp.float32))
    learner_caption_grid = unit_rows(learner_caption_vectors.astype(jnp.float32))
    mentor_caption_grid = unit_rows(mentor_caption_vectors.astype(jnp.float32))
    learner_network = jnp.dot(learner_vector_list, learner_caption_grid.T, preferred_element_type=jnp.float32) / logit_divisor
    mentor_network = jnp.dot(mentor_vector_list, mentor_caption_grid.T, preferred_element_type=jnp.float32) / logit_divisor
    log_student = log_total(learner_network)
    log_teacher = log_total(mentor_network)
    probs = jnp.exp(mentor_network - log_teacher[:, None])
    cross_sum = lax.optimization_barrier(jnp.sum(probs * (mentor_network - learner_network), 1))
    label_score = jnp.take_along_axis(learner_network, matching_caption_slot[:, None].astype(jnp.int32), 1)[:, 0]
    losses = cross_sum - log_teacher + 2.0 * log_student - label_score
    return (block_out, embedding, losses)
```

```python
import jax
import jax.numpy as jnp
from jax import lax
from jax.sharding import PartitionSpec as P

SIDE = 8
KERNEL = 7


EPSILON = 1e-06
HIGHEST = lax.Precision.HIGHEST


def depthwise(incoming_feature_maps, spatial_filter_tensor, spatial_filter_offset):
    radius = KERNEL // 2
    padded = jnp.pad(
        incoming_feature_maps.astype(jnp.float32),
        ((0, 0), (radius, radius), (radius, radius), (0, 0)),
    )
    summed = jnp.zeros(incoming_feature_maps.shape, jnp.float32)
    for vertical in range(KERNEL):
        for horizontal in range(KERNEL):
            window = padded[:, vertical : vertical + SIDE, horizontal : horizontal + SIDE, :]
            summed = (
                summed + spatial_filter_tensor[vertical, horizontal].astype(jnp.float32) * window
            )
    return (summed + spatial_filter_offset).astype(jnp.bfloat16)


def unit_rows(values):
    return (values / jnp.sqrt(jnp.sum(values * values, -1, keepdims=True) + EPSILON)).astype(
        jnp.bfloat16
    )


def logits(queries, keys, divisor):
    return (
        lax.dot_general(
            queries, keys, (((1,), (1,)), ((), ())), preferred_element_type=jnp.float32
        )
        / divisor
    )


def broadcast_gather(value, axis):
    copies = jnp.broadcast_to(value[None], (lax.axis_size(axis),) + value.shape)
    return lax.all_to_all(copies, axis, 0, 0)


def split_product(values, weights):
    top = lax.reduce_precision(values, 8, 7)
    rest = values - top
    middle = lax.reduce_precision(rest, 8, 7)
    pieces = jnp.concatenate([top, middle, rest - middle], 0).astype(jnp.bfloat16)
    product = jnp.dot(pieces, weights, preferred_element_type=jnp.float32)
    rows = values.shape[0]
    return product[2 * rows :] + product[rows : 2 * rows] + product[:rows]


def on_device(
    incoming_feature_maps,
    spatial_filter_tensor,
    spatial_filter_offset,
    unit_layernorm_multiplier,
    unit_layernorm_offset_vector,
    expansion_linear_map,
    expansion_offset,
    contraction_linear_map,
    contraction_offset,
    residual_channel_factor,
    readout_layernorm_multiplier,
    readout_layernorm_offset,
    readout_linear_map,
    learner_caption_vectors,
    mentor_caption_vectors,
    mentor_picture_vectors,
    divisor_per_slot,
    active_program_slot,
    matching_caption_slot,
):
    group_count = incoming_feature_maps.shape[0]
    local_width = incoming_feature_maps.shape[3]
    shard_count = lax.axis_size("fsdp")
    shard_index = lax.axis_index("fsdp")
    data_index = lax.axis_index("dp")
    full_width = local_width * shard_count
    token_rows = group_count * SIDE * SIDE
    logit_divisor = lax.dynamic_index_in_dim(
        divisor_per_slot, active_program_slot[0], keepdims=False
    )
    key_count = learner_caption_vectors.shape[0]
    teacher_rows = broadcast_gather(unit_rows(mentor_picture_vectors.astype(jnp.float32)), "dp")
    teacher_part = logits(
        teacher_rows.reshape(-1, teacher_rows.shape[2]),
        unit_rows(mentor_caption_vectors.astype(jnp.float32)),
        logit_divisor,
    )
    teacher = lax.all_to_all(
        teacher_part.reshape(lax.axis_size("dp"), group_count, key_count), "dp", 0, 0
    )
    teacher = jnp.swapaxes(teacher, 0, 1).reshape(group_count, -1)
    top_teacher = jnp.max(teacher, 1, keepdims=True)
    teacher_weights = jnp.exp(teacher - top_teacher)
    sum_teacher = jnp.sum(teacher_weights, 1)
    student_keys = lax.all_gather(
        unit_rows(learner_caption_vectors.astype(jnp.float32)), "dp", axis=0, tiled=True
    )
    readout_full = lax.all_gather(readout_linear_map, "fsdp", axis=0, tiled=True)
    head_params = broadcast_gather(
        jnp.stack([readout_layernorm_multiplier, readout_layernorm_offset]), "fsdp"
    )
    head_gain = head_params[:, 0].reshape(full_width)
    head_shift = head_params[:, 1].reshape(full_width)
    convolved = depthwise(incoming_feature_maps, spatial_filter_tensor, spatial_filter_offset)
    values = convolved.astype(jnp.float32).reshape(token_rows, local_width)
    totals, squares = lax.psum((jnp.sum(values, 1), jnp.sum(values * values, 1)), "fsdp")
    mean_val = totals / full_width
    spread = squares / full_width - mean_val * mean_val
    gain_part = lax.dynamic_slice_in_dim(
        unit_layernorm_multiplier, shard_index * local_width, local_width
    )
    shift_part = lax.dynamic_slice_in_dim(
        unit_layernorm_offset_vector, shard_index * local_width, local_width
    )
    local_normed = (
        (values - mean_val[:, None]) / jnp.sqrt(spread[:, None] + EPSILON) * gain_part + shift_part
    ).astype(jnp.bfloat16)
    normed = lax.all_gather(local_normed, "fsdp", axis=1, tiled=True)
    preact = (
        jnp.dot(
            normed,
            lax.all_gather(expansion_linear_map, "dp", axis=0, tiled=True),
            preferred_element_type=jnp.float32,
        )
        + expansion_offset
    )
    hidden = jax.nn.gelu(preact, approximate=False).astype(jnp.bfloat16)
    partials = jnp.dot(
        hidden,
        lax.all_gather(contraction_linear_map, "dp", axis=1, tiled=True),
        preferred_element_type=jnp.float32,
    )
    branch = lax.psum_scatter(
        partials.astype(jnp.bfloat16), "fsdp", scatter_dimension=1, tiled=True
    ).astype(jnp.float32)
    residual = incoming_feature_maps.astype(jnp.float32).reshape(token_rows, local_width)
    block_out = (
        (residual + residual_channel_factor * (branch + contraction_offset))
        .astype(jnp.bfloat16)
        .reshape(incoming_feature_maps.shape)
    )
    pooled = jnp.mean(
        block_out.astype(jnp.float32).reshape(group_count, SIDE * SIDE, local_width), 1
    )
    pooled_full = broadcast_gather(pooled, "fsdp")
    pooled_full = jnp.swapaxes(pooled_full, 0, 1).reshape(group_count, full_width)
    mean_val = jnp.mean(pooled_full, 1, keepdims=True)
    centered = pooled_full - mean_val
    spread = jnp.mean(centered * centered, 1, keepdims=True)
    head_normed = centered / jnp.sqrt(spread + EPSILON) * head_gain + head_shift
    embedding = split_product(head_normed, readout_full)
    student = logits(unit_rows(embedding), student_keys, logit_divisor)
    local_columns = lax.iota(jnp.int32, student.shape[1])
    column_ids = (
        local_columns // key_count * shard_count + shard_index
    ) * key_count + local_columns % key_count
    labels = lax.dynamic_slice_in_dim(matching_caption_slot, data_index * group_count, group_count)
    top_student = jnp.max(student, 1, keepdims=True)
    sum_student = jnp.sum(jnp.exp(student - top_student), 1)
    label_score = jnp.sum(jnp.where(labels[:, None] == column_ids[None, :], student, 0.0), 1)
    cross_sum = jnp.sum(teacher_weights * (teacher - student), 1)
    stats = jnp.stack(
        [top_student[:, 0], sum_student, top_teacher[:, 0], sum_teacher, cross_sum, label_score], 1
    )
    per_device = group_count // shard_count
    stats = lax.all_to_all(stats.reshape(shard_count, per_device, 6), "fsdp", 0, 0)
    top_s, sum_s, top_t, sum_t, cross, label = [stats[:, :, member] for member in range(6)]
    best_s = jnp.max(top_s, 0)
    best_t = jnp.max(top_t, 0)
    scale_t = jnp.exp(top_t - best_t)
    total_t = jnp.sum(sum_t * scale_t, 0)
    log_student = best_s + jnp.log(jnp.sum(sum_s * jnp.exp(top_s - best_s), 0))
    losses = (
        jnp.sum(cross * scale_t, 0) / total_t
        - (best_t + jnp.log(total_t))
        + 2.0 * log_student
        - jnp.sum(label, 0)
    )
    return (block_out, embedding, losses)


def solution(mesh):
    placed = (
        P("dp", None, None, "fsdp"),
        P(None, None, "fsdp"),
        P("fsdp"),
        P(),
        P(),
        P("dp", "fsdp"),
        P("fsdp"),
        P("fsdp", "dp"),
        P("fsdp"),
        P("fsdp"),
        P("fsdp"),
        P("fsdp"),
        P("fsdp", None),
        P(("dp", "fsdp"), None),
        P(("dp", "fsdp"), None),
        P("dp", None),
        P(),
        P(),
        P(),
    )
    return jax.shard_map(
        on_device,
        mesh=mesh,
        in_specs=placed,
        out_specs=(P("dp", None, None, "fsdp"), P("dp", None), P(("dp", "fsdp"))),
        check_vma=False,
    )
```

```python
import jax
import jax.numpy as jnp
from jax import lax
from jax.sharding import PartitionSpec as P

SIDE = 8
KERNEL = 7
Z_SIDE = 8
X_SIDE = 4
Y_SIDE = 4
CORES = 2
X_GROUPS = [[z * X_SIDE + x for x in range(X_SIDE)] for z in range(Z_SIDE)]
Z_GROUPS = [[z * X_SIDE + x for z in range(Z_SIDE)] for x in range(X_SIDE)]


EPSILON = 1e-06
HIGHEST = lax.Precision.HIGHEST


def depthwise(incoming_feature_maps, spatial_filter_tensor, spatial_filter_offset):
    radius = KERNEL // 2
    padded = jnp.pad(
        incoming_feature_maps.astype(jnp.float32),
        ((0, 0), (radius, radius), (radius, radius), (0, 0)),
    )
    summed = jnp.zeros(incoming_feature_maps.shape, jnp.float32)
    for vertical in range(KERNEL):
        for horizontal in range(KERNEL):
            window = padded[:, vertical : vertical + SIDE, horizontal : horizontal + SIDE, :]
            summed = (
                summed + spatial_filter_tensor[vertical, horizontal].astype(jnp.float32) * window
            )
    return (summed + spatial_filter_offset).astype(jnp.bfloat16)


def unit_rows(values):
    return (values / jnp.sqrt(jnp.sum(values * values, -1, keepdims=True) + EPSILON)).astype(
        jnp.bfloat16
    )


def logits(queries, keys, divisor):
    return (
        lax.dot_general(
            queries, keys, (((1,), (1,)), ((), ())), preferred_element_type=jnp.float32
        )
        / divisor
    )


def broadcast_gather(value, axis):
    copies = jnp.broadcast_to(value[None], (lax.axis_size(axis),) + value.shape)
    return lax.all_to_all(copies, axis, 0, 0)


def split_product(values, weights):
    top = lax.reduce_precision(values, 8, 7)
    rest = values - top
    middle = lax.reduce_precision(rest, 8, 7)
    pieces = jnp.concatenate([top, middle, rest - middle], 0).astype(jnp.bfloat16)
    product = jnp.dot(pieces, weights, preferred_element_type=jnp.float32)
    rows = values.shape[0]
    return product[2 * rows :] + product[rows : 2 * rows] + product[:rows]


def ring_pairs(size, inner, step):
    block = size // inner
    return [
        (outer * inner + place, (outer + step) % block * inner + place)
        for outer in range(block)
        for place in range(inner)
    ]


def inner_pairs(size, inner, step):
    return [
        (outer * inner + place, outer * inner + (place + step) % inner)
        for outer in range(size // inner)
        for place in range(inner)
    ]


def send_z(value, step):
    return lax.ppermute(value, "dp", ring_pairs(Z_SIDE * X_SIDE, X_SIDE, step))


def send_x(value, step):
    return lax.ppermute(value, "dp", inner_pairs(Z_SIDE * X_SIDE, X_SIDE, step))


def send_y(value, step):
    return lax.ppermute(value, "fsdp", ring_pairs(Y_SIDE * CORES, CORES, step))


def swap_cores(value):
    return lax.ppermute(value, "fsdp", inner_pairs(Y_SIDE * CORES, CORES, 1))


def both_ways(value, send):
    return send(value, 1), send(value, -1)


def both_halves(before, after, send):
    half = before.shape[0] // 2
    return send(before[:half], 1), send(after[half:], -1)


def fence(*values):
    return lax.optimization_barrier(values)


def scatter_sums(partials, y_index, core_index):
    def of(member):
        return lax.dynamic_index_in_dim(partials, member, 0, keepdims=False)

    others = jnp.stack([of(2 * y + 1 - core_index) for y in range(Y_SIDE)])
    received = swap_cores(others)

    def both(step):
        place = (y_index + step) % Y_SIDE
        mine = of(2 * place + core_index).astype(jnp.float32)
        return mine + lax.dynamic_index_in_dim(received, place, 0, keepdims=False)

    half = partials.shape[1] // 2
    far = both(2).astype(jnp.bfloat16)
    from_below = send_y(far[:half], 1)
    from_above = send_y(far[half:], -1)
    following = both(1)
    following = jnp.concatenate([following[:half] + from_below, following[half:]], 0)
    previous = both(3)
    previous = jnp.concatenate([previous[:half], previous[half:] + from_above], 0)
    below = send_y(following.astype(jnp.bfloat16), 1)
    above = send_y(previous.astype(jnp.bfloat16), -1)
    return both(0) + below + above


def on_device(
    incoming_feature_maps,
    spatial_filter_tensor,
    spatial_filter_offset,
    unit_layernorm_multiplier,
    unit_layernorm_offset_vector,
    expansion_linear_map,
    expansion_offset,
    contraction_linear_map,
    contraction_offset,
    residual_channel_factor,
    readout_layernorm_multiplier,
    readout_layernorm_offset,
    readout_linear_map,
    learner_caption_vectors,
    mentor_caption_vectors,
    mentor_picture_vectors,
    divisor_per_slot,
    active_program_slot,
    matching_caption_slot,
):
    group_count = incoming_feature_maps.shape[0]
    local_width = incoming_feature_maps.shape[3]
    shard_count = lax.axis_size("fsdp")
    shard_index = lax.axis_index("fsdp")
    data_index = lax.axis_index("dp")
    z_index = data_index // X_SIDE
    x_index = data_index % X_SIDE
    y_index = shard_index // CORES
    core_index = shard_index % CORES
    full_width = local_width * shard_count
    token_rows = group_count * SIDE * SIDE
    key_count = learner_caption_vectors.shape[0]
    second_rows = contraction_linear_map.shape[1]
    logit_divisor = lax.dynamic_index_in_dim(
        divisor_per_slot, active_program_slot[0], keepdims=False
    )

    part_rows = second_rows // 2
    own_parts = [
        lax.all_gather(part, "dp", axis=0, tiled=True, axis_index_groups=Z_GROUPS)
        for part in (contraction_linear_map.T[:part_rows], contraction_linear_map.T[part_rows:])
    ]
    near = both_ways(expansion_linear_map, send_x)
    near, features = fence(near, incoming_feature_maps)

    far = both_halves(*near, send_x)
    convolved = depthwise(features, spatial_filter_tensor, spatial_filter_offset)
    values = convolved.astype(jnp.float32).reshape(token_rows, local_width)
    sums = jnp.stack([jnp.sum(values, 1), jnp.sum(values * values, 1)])

    def placed(buffer, part, step):
        return lax.dynamic_update_index_in_dim(buffer, part, (x_index + step) % X_SIDE, 0)

    block = jnp.zeros((X_SIDE,) + expansion_linear_map.shape, jnp.bfloat16)
    block = placed(placed(placed(block, expansion_linear_map, 0), near[1], 1), near[0], 3)
    far, convolved, sums, block = fence(far, convolved, sums, block)

    block = placed(block, jnp.concatenate(far, 0), 2)
    first = {0: block.reshape(-1, block.shape[2])}
    first[7], first[1] = both_ways(first[0], send_z)
    near_parts = [both_ways(own_parts[0], send_x)]
    totals, squares = jnp.sum(broadcast_gather(sums, "fsdp"), 0)
    mean_val = totals / full_width
    spread = squares / full_width - mean_val * mean_val
    gain_part = lax.dynamic_slice_in_dim(
        unit_layernorm_multiplier, shard_index * local_width, local_width
    )
    shift_part = lax.dynamic_slice_in_dim(
        unit_layernorm_offset_vector, shard_index * local_width, local_width
    )
    values = convolved.astype(jnp.float32).reshape(token_rows, local_width)
    local_normed = (
        (values - mean_val[:, None]) / jnp.sqrt(spread[:, None] + EPSILON) * gain_part + shift_part
    ).astype(jnp.bfloat16)
    head_rows = jnp.stack([readout_layernorm_multiplier, readout_layernorm_offset])
    head_rows = split_product(head_rows, readout_linear_map)
    teacher_rows = unit_rows(mentor_picture_vectors.astype(jnp.float32))
    own_keys = jnp.concatenate(
        [
            unit_rows(keys.astype(jnp.float32))
            for keys in (learner_caption_vectors, mentor_caption_vectors)
        ],
        1,
    )
    first, head_rows, teacher_rows, own_keys, near_parts, own_parts[0], local_normed = fence(
        first, head_rows, teacher_rows, own_keys, near_parts, own_parts[0], local_normed
    )

    first[6], first[2] = send_z(first[7], 1), send_z(first[1], -1)
    normed = lax.all_gather(local_normed, "fsdp", axis=0)
    near_parts.append(both_ways(own_parts[1], send_x))
    first, own_keys = fence(first, own_keys)

    def first_product(place):
        part = lax.dynamic_index_in_dim(normed, (z_index + place) % Z_SIDE, 0, keepdims=False)
        return jnp.dot(part, first[place], preferred_element_type=jnp.float32)

    first[5], first[3] = send_z(first[6], 1), send_z(first[2], -1)
    all_keys = lax.all_gather(own_keys, "dp", axis=0, tiled=True)
    far_parts = [both_halves(*near_parts[0], send_x)]
    preact = first_product(0) + expansion_offset
    for place in (1, 7):
        preact = preact + first_product(place)
    first, far_parts, near_parts, preact = fence(first, far_parts, near_parts, preact)

    step = both_halves(first[5], first[3], send_z)
    far_parts.append(both_halves(*near_parts[1], send_x))
    for place in (2, 6, 3, 5):
        preact = preact + first_product(place)
    step, preact, far_parts = fence(step, preact, far_parts)
    far_parts = [jnp.concatenate(far, 0) for far in far_parts]
    first[4] = jnp.concatenate(step, 0)
    preact = preact + first_product(4)
    hidden = jax.nn.gelu(preact, approximate=False).astype(jnp.bfloat16)

    summed = []
    for piece in (
        own_parts
        + [near[1] for near in near_parts]
        + far_parts
        + [near[0] for near in near_parts]
    ):
        partials = lax.dot_general(
            piece, hidden, (((1,), (1,)), ((), ())), preferred_element_type=jnp.float32
        ).astype(jnp.bfloat16)
        summed.append(partials.reshape(Z_SIDE, part_rows, token_rows))
    summed = jnp.concatenate(summed, 1)
    branch = scatter_sums(summed, y_index, core_index)
    branch = jnp.roll(branch.reshape(X_SIDE, second_rows, token_rows), x_index, 0)
    branch = branch.reshape(local_width, token_rows).T
    residual = incoming_feature_maps.astype(jnp.float32).reshape(token_rows, local_width)
    block_out = (
        (residual + residual_channel_factor * (branch + contraction_offset))
        .astype(jnp.bfloat16)
        .reshape(incoming_feature_maps.shape)
    )
    pooled = jnp.mean(
        block_out.astype(jnp.float32).reshape(group_count, SIDE * SIDE, local_width), 1
    )
    local_mean = jnp.mean(pooled, 1, keepdims=True)
    centered = pooled - local_mean
    local_square = jnp.sum(centered * centered, 1, keepdims=True)
    product = split_product(centered * readout_layernorm_multiplier, readout_linear_map)
    local_stats = jnp.concatenate([local_mean, local_square], 1).reshape(1, -1)
    local_stats = jnp.pad(local_stats, ((0, 0), (0, product.shape[1] - local_stats.shape[1])))
    shares = broadcast_gather(jnp.concatenate([product, head_rows, local_stats], 0), "fsdp")
    shares, all_keys = fence(shares, all_keys)
    head_stats = shares[:, group_count + 2, : 2 * group_count].reshape(shard_count, group_count, 2)
    means, head_squares = head_stats[:, :, 0], head_stats[:, :, 1]
    mean_val = jnp.mean(means, 0)
    offsets = means - mean_val
    spread = jnp.sum(head_squares + local_width * (offsets * offsets), 0) / full_width
    scaled = jnp.sum(
        shares[:, :group_count] + offsets[:, :, None] * shares[:, group_count, None, :], 0
    )
    embedding = scaled / jnp.sqrt(spread[:, None] + EPSILON) + jnp.sum(shares[:, group_count + 1], 0)
    student_rows = unit_rows(embedding)
    width = student_rows.shape[1]
    teacher = logits(teacher_rows, all_keys[:, width:], logit_divisor)
    top_teacher = jnp.max(teacher, 1, keepdims=True)
    teacher_weights = jnp.exp(teacher - top_teacher)
    sum_teacher = jnp.sum(teacher_weights, 1)
    student = logits(student_rows, all_keys[:, :width], logit_divisor)
    local_columns = lax.iota(jnp.int32, student.shape[1])
    column_ids = (
        local_columns // key_count * shard_count + shard_index
    ) * key_count + local_columns % key_count
    labels = lax.dynamic_slice_in_dim(matching_caption_slot, data_index * group_count, group_count)
    top_student = jnp.max(student, 1, keepdims=True)
    sum_student = jnp.sum(jnp.exp(student - top_student), 1)
    label_score = jnp.sum(jnp.where(labels[:, None] == column_ids[None, :], student, 0.0), 1)
    cross_sum = jnp.sum(teacher_weights * (teacher - student), 1)
    stats = jnp.stack(
        [top_student[:, 0], sum_student, top_teacher[:, 0], sum_teacher, cross_sum, label_score], 1
    )
    per_device = group_count // shard_count
    stats = lax.all_to_all(stats.reshape(shard_count, per_device, 6), "fsdp", 0, 0)
    top_s, sum_s, top_t, sum_t, cross, label = [stats[:, :, member] for member in range(6)]
    best_s = jnp.max(top_s, 0)
    best_t = jnp.max(top_t, 0)
    scale_t = jnp.exp(top_t - best_t)
    total_t = jnp.sum(sum_t * scale_t, 0)
    log_student = best_s + jnp.log(jnp.sum(sum_s * jnp.exp(top_s - best_s), 0))
    losses = (
        jnp.sum(cross * scale_t, 0) / total_t
        - (best_t + jnp.log(total_t))
        + 2.0 * log_student
        - jnp.sum(label, 0)
    )
    return (block_out, embedding, losses)


def solution(mesh):
    placed = (
        P("dp", None, None, "fsdp"),
        P(None, None, "fsdp"),
        P("fsdp"),
        P(),
        P(),
        P("dp", "fsdp"),
        P("fsdp"),
        P("fsdp", "dp"),
        P("fsdp"),
        P("fsdp"),
        P("fsdp"),
        P("fsdp"),
        P("fsdp", None),
        P(("dp", "fsdp"), None),
        P(("dp", "fsdp"), None),
        P("dp", None),
        P(),
        P(),
        P(),
    )
    return jax.shard_map(
        on_device,
        mesh=mesh,
        in_specs=placed,
        out_specs=(P("dp", None, None, "fsdp"), P("dp", None), P(("dp", "fsdp"))),
        check_vma=False,
    )
```

```python
import jax
import jax.numpy as jnp
from jax import lax
from jax.experimental import pallas as pl
from jax.experimental.pallas import tpu as pltpu
from jax.sharding import PartitionSpec as P

SIDE = 8
KERNEL = 7
Z_SIDE = 8
X_SIDE = 4
Y_SIDE = 4
CORES = 2
X_GROUPS = [[z * X_SIDE + x for x in range(X_SIDE)] for z in range(Z_SIDE)]
Z_GROUPS = [[z * X_SIDE + x for z in range(Z_SIDE)] for x in range(X_SIDE)]


EPSILON = 1e-06
HIGHEST = lax.Precision.HIGHEST


def depthwise(incoming_feature_maps, spatial_filter_tensor, spatial_filter_offset):
    radius = KERNEL // 2
    padded = jnp.pad(
        incoming_feature_maps.astype(jnp.float32),
        ((0, 0), (radius, radius), (radius, radius), (0, 0)),
    )
    summed = jnp.zeros(incoming_feature_maps.shape, jnp.float32)
    for vertical in range(KERNEL):
        for horizontal in range(KERNEL):
            window = padded[:, vertical : vertical + SIDE, horizontal : horizontal + SIDE, :]
            summed = (
                summed + spatial_filter_tensor[vertical, horizontal].astype(jnp.float32) * window
            )
    return (summed + spatial_filter_offset).astype(jnp.bfloat16)


def unit_rows(values):
    return (values / jnp.sqrt(jnp.sum(values * values, -1, keepdims=True) + EPSILON)).astype(
        jnp.bfloat16
    )


def logits(queries, keys, divisor):
    return (
        lax.dot_general(
            queries, keys, (((1,), (1,)), ((), ())), preferred_element_type=jnp.float32
        )
        / divisor
    )


def broadcast_gather(value, axis):
    copies = jnp.broadcast_to(value[None], (lax.axis_size(axis),) + value.shape)
    return lax.all_to_all(copies, axis, 0, 0)


def split_product(values, weights):
    top = lax.reduce_precision(values, 8, 7)
    rest = values - top
    middle = lax.reduce_precision(rest, 8, 7)
    pieces = jnp.concatenate([top, middle, rest - middle], 0).astype(jnp.bfloat16)
    product = jnp.dot(pieces, weights, preferred_element_type=jnp.float32)
    rows = values.shape[0]
    return product[2 * rows :] + product[rows : 2 * rows] + product[:rows]


def ring_pairs(size, inner, step):
    block = size // inner
    return [
        (outer * inner + place, (outer + step) % block * inner + place)
        for outer in range(block)
        for place in range(inner)
    ]


def inner_pairs(size, inner, step):
    return [
        (outer * inner + place, outer * inner + (place + step) % inner)
        for outer in range(size // inner)
        for place in range(inner)
    ]


def send_z(value, step):
    return lax.ppermute(value, "dp", ring_pairs(Z_SIDE * X_SIDE, X_SIDE, step))


def send_x(value, step):
    return lax.ppermute(value, "dp", inner_pairs(Z_SIDE * X_SIDE, X_SIDE, step))


def send_y(value, step):
    return lax.ppermute(value, "fsdp", ring_pairs(Y_SIDE * CORES, CORES, step))


def swap_cores(value):
    return lax.ppermute(value, "fsdp", inner_pairs(Y_SIDE * CORES, CORES, 1))


def both_ways(value, send):
    return send(value, 1), send(value, -1)


def both_halves(before, after, send):
    half = before.shape[0] // 2
    return send(before[:half], 1), send(after[half:], -1)


def fence(*values):
    return lax.optimization_barrier(values)


def second_kernel(hidden_ref, *rest):
    sources = rest[: 2 * X_SIDE]
    kept_ref, sent_ref, blocks, flipped, arrived = rest[2 * X_SIDE :]
    core = lax.axis_index("fsdp") % CORES
    rows = blocks.shape[1]
    members = Z_SIDE // 2
    copies = [
        pltpu.make_async_copy(source, blocks.at[place], arrived.at[place])
        for place, source in enumerate(sources)
    ]
    for copy in copies:
        copy.start()
    flipped[...] = hidden_ref[...].T
    for place, copy in enumerate(copies):
        copy.wait()
        product = jnp.dot(blocks[place], flipped[...], preferred_element_type=jnp.float32)
        product = product.reshape(members, rows // members, -1)
        for pair in range(members // CORES):
            y = place % 2 * (members // CORES) + pair
            first, second = product[CORES * pair], product[CORES * pair + 1]
            kept_ref[y, place // 2] = jnp.where(core == 0, first, second).astype(jnp.bfloat16)
            sent_ref[y, place // 2] = jnp.where(core == 0, second, first).astype(jnp.bfloat16)


def second_products(hidden, *blocks):
    tokens, depth = hidden.shape
    rows = blocks[0].shape[0]
    part = jax.ShapeDtypeStruct(
        (Y_SIDE, X_SIDE, 2 * rows // Z_SIDE, tokens), jnp.bfloat16
    )
    whole = pl.BlockSpec(memory_space=pltpu.VMEM)
    apart = pl.BlockSpec(memory_space=pl.ANY)
    kept, sent = pl.pallas_call(
        second_kernel,
        out_shape=(part, part),
        in_specs=[whole] + [apart] * len(blocks),
        out_specs=(whole, whole),
        scratch_shapes=[
            pltpu.VMEM((8, rows, depth), jnp.bfloat16),
            pltpu.VMEM((depth, tokens), jnp.bfloat16),
            pltpu.SemaphoreType.DMA((8,)),
        ],
        compiler_params=pltpu.CompilerParams(vmem_limit_bytes=40 * 1024 * 1024),
        cost_estimate=pl.CostEstimate(
            flops=16 * rows * depth * tokens, bytes_accessed=20 * rows * depth, transcendentals=0
        ),
    )(hidden, *blocks)
    shape = (Y_SIDE, -1, tokens)
    return kept.reshape(shape), sent.reshape(shape)


def scatter_sums(kept, sent, y_index):
    received = swap_cores(sent)

    def both(step):
        place = (y_index + step) % Y_SIDE
        mine = lax.dynamic_index_in_dim(kept, place, 0, keepdims=False).astype(jnp.float32)
        return mine + lax.dynamic_index_in_dim(received, place, 0, keepdims=False)

    half = kept.shape[1] // 2
    far = both(2).astype(jnp.bfloat16)
    from_below = send_y(far[:half], 1)
    from_above = send_y(far[half:], -1)
    following = both(1)
    following = jnp.concatenate([following[:half] + from_below, following[half:]], 0)
    previous = both(3)
    previous = jnp.concatenate([previous[:half], previous[half:] + from_above], 0)
    below = send_y(following.astype(jnp.bfloat16), 1)
    above = send_y(previous.astype(jnp.bfloat16), -1)
    return both(0) + below + above


def on_device(
    incoming_feature_maps,
    spatial_filter_tensor,
    spatial_filter_offset,
    unit_layernorm_multiplier,
    unit_layernorm_offset_vector,
    expansion_linear_map,
    expansion_offset,
    contraction_linear_map,
    contraction_offset,
    residual_channel_factor,
    readout_layernorm_multiplier,
    readout_layernorm_offset,
    readout_linear_map,
    learner_caption_vectors,
    mentor_caption_vectors,
    mentor_picture_vectors,
    divisor_per_slot,
    active_program_slot,
    matching_caption_slot,
):
    group_count = incoming_feature_maps.shape[0]
    local_width = incoming_feature_maps.shape[3]
    shard_count = lax.axis_size("fsdp")
    shard_index = lax.axis_index("fsdp")
    data_index = lax.axis_index("dp")
    z_index = data_index // X_SIDE
    x_index = data_index % X_SIDE
    y_index = shard_index // CORES
    full_width = local_width * shard_count
    token_rows = group_count * SIDE * SIDE
    key_count = learner_caption_vectors.shape[0]
    second_rows = contraction_linear_map.shape[1]
    logit_divisor = lax.dynamic_index_in_dim(
        divisor_per_slot, active_program_slot[0], keepdims=False
    )

    own_x = lax.all_gather(
        contraction_linear_map.T, "dp", axis=0, tiled=True, axis_index_groups=Z_GROUPS
    )
    around = [send_x(expansion_linear_map, step) for step in (-1, 2, 1)]
    convolved = depthwise(incoming_feature_maps, spatial_filter_tensor, spatial_filter_offset)
    values = convolved.astype(jnp.float32).reshape(token_rows, local_width)
    sums = jnp.stack([jnp.sum(values, 1), jnp.sum(values * values, 1)])
    around, convolved, sums = fence(around, convolved, sums)

    def placed(buffer, part, step):
        return lax.dynamic_update_index_in_dim(buffer, part, (x_index + step) % X_SIDE, 0)

    block = jnp.zeros((X_SIDE,) + expansion_linear_map.shape, jnp.bfloat16)
    for step, part in enumerate([expansion_linear_map] + around):
        block = placed(block, part, step)
    first = {0: block.reshape(-1, block.shape[2])}
    first[7], first[1] = both_ways(first[0], send_z)
    totals, squares = jnp.sum(broadcast_gather(sums, "fsdp"), 0)
    mean_val = totals / full_width
    spread = squares / full_width - mean_val * mean_val
    gain_part = lax.dynamic_slice_in_dim(
        unit_layernorm_multiplier, shard_index * local_width, local_width
    )
    shift_part = lax.dynamic_slice_in_dim(
        unit_layernorm_offset_vector, shard_index * local_width, local_width
    )
    values = convolved.astype(jnp.float32).reshape(token_rows, local_width)
    local_normed = (
        (values - mean_val[:, None]) / jnp.sqrt(spread[:, None] + EPSILON) * gain_part + shift_part
    ).astype(jnp.bfloat16)
    head_rows = jnp.stack([readout_layernorm_multiplier, readout_layernorm_offset])
    head_rows = split_product(head_rows, readout_linear_map)
    teacher_rows = unit_rows(mentor_picture_vectors.astype(jnp.float32))
    own_keys = jnp.concatenate(
        [
            unit_rows(keys.astype(jnp.float32))
            for keys in (learner_caption_vectors, mentor_caption_vectors)
        ],
        1,
    )
    part_rows = own_x.shape[0] // 2
    own_low, own_high = own_x[:part_rows], own_x[part_rows:]
    first, head_rows, teacher_rows, own_keys, local_normed, own_low, own_high = fence(
        first, head_rows, teacher_rows, own_keys, local_normed, own_low, own_high
    )

    near_low = both_ways(own_low, send_x)
    first[6], first[2] = send_z(first[7], 1), send_z(first[1], -1)
    normed = lax.all_gather(local_normed, "fsdp", axis=0)
    first, near_low, own_keys = fence(first, near_low, own_keys)

    near_high = both_ways(own_high, send_x)
    far_low = send_x(near_low[0], 1)
    first[5], first[3] = send_z(first[6], 1), send_z(first[2], -1)
    all_keys = lax.all_gather(own_keys, "dp", axis=0, tiled=True)

    def first_product(place):
        part = lax.dynamic_index_in_dim(normed, (z_index + place) % Z_SIDE, 0, keepdims=False)
        return jnp.dot(part, first[place], preferred_element_type=jnp.float32)

    preact = first_product(0) + expansion_offset
    for place in (1, 7, 2, 6):
        preact = preact + first_product(place)
    first, near_high, preact = fence(first, near_high, preact)

    far_high = send_x(near_high[1], -1)
    step = both_halves(first[5], first[3], send_z)
    for place in (3, 5):
        preact = preact + first_product(place)
    step, preact, far_low, far_high = fence(step, preact, far_low, far_high)
    first[4] = jnp.concatenate(step, 0)
    preact = preact + first_product(4)
    hidden = jax.nn.gelu(preact, approximate=False).astype(jnp.bfloat16)

    blocks = (own_low, own_high, near_low[1], near_high[1], far_low, far_high)
    kept, sent = second_products(hidden, *blocks, near_low[0], near_high[0])
    branch = scatter_sums(kept, sent, y_index)
    branch = jnp.roll(branch.reshape(X_SIDE, second_rows, token_rows), x_index, 0)
    branch = branch.reshape(local_width, token_rows).T
    residual = incoming_feature_maps.astype(jnp.float32).reshape(token_rows, local_width)
    block_out = (
        (residual + residual_channel_factor * (branch + contraction_offset))
        .astype(jnp.bfloat16)
        .reshape(incoming_feature_maps.shape)
    )
    pooled = jnp.mean(
        block_out.astype(jnp.float32).reshape(group_count, SIDE * SIDE, local_width), 1
    )
    local_mean = jnp.mean(pooled, 1, keepdims=True)
    centered = pooled - local_mean
    local_square = jnp.sum(centered * centered, 1, keepdims=True)
    product = split_product(centered * readout_layernorm_multiplier, readout_linear_map)
    local_stats = jnp.concatenate([local_mean, local_square], 1).reshape(1, -1)
    local_stats = jnp.pad(local_stats, ((0, 0), (0, product.shape[1] - local_stats.shape[1])))
    shares = broadcast_gather(jnp.concatenate([product, head_rows, local_stats], 0), "fsdp")
    head_stats = shares[:, group_count + 2, : 2 * group_count].reshape(shard_count, group_count, 2)
    means, head_squares = head_stats[:, :, 0], head_stats[:, :, 1]
    mean_val = jnp.mean(means, 0)
    offsets = means - mean_val
    spread = jnp.sum(head_squares + local_width * (offsets * offsets), 0) / full_width
    scaled = jnp.sum(
        shares[:, :group_count] + offsets[:, :, None] * shares[:, group_count, None, :], 0
    )
    embedding = scaled / jnp.sqrt(spread[:, None] + EPSILON) + jnp.sum(shares[:, group_count + 1], 0)
    student_rows = unit_rows(embedding)
    width = student_rows.shape[1]
    teacher = logits(teacher_rows, all_keys[:, width:], logit_divisor)
    top_teacher = jnp.max(teacher, 1, keepdims=True)
    teacher_weights = jnp.exp(teacher - top_teacher)
    sum_teacher = jnp.sum(teacher_weights, 1)
    student = logits(student_rows, all_keys[:, :width], logit_divisor)
    local_columns = lax.iota(jnp.int32, student.shape[1])
    column_ids = (
        local_columns // key_count * shard_count + shard_index
    ) * key_count + local_columns % key_count
    labels = lax.dynamic_slice_in_dim(matching_caption_slot, data_index * group_count, group_count)
    top_student = jnp.max(student, 1, keepdims=True)
    sum_student = jnp.sum(jnp.exp(student - top_student), 1)
    label_score = jnp.sum(jnp.where(labels[:, None] == column_ids[None, :], student, 0.0), 1)
    cross_sum = jnp.sum(teacher_weights * (teacher - student), 1)
    stats = jnp.stack(
        [top_student[:, 0], sum_student, top_teacher[:, 0], sum_teacher, cross_sum, label_score], 1
    )
    per_device = group_count // shard_count
    stats = lax.all_to_all(stats.reshape(shard_count, per_device, 6), "fsdp", 0, 0)
    top_s, sum_s, top_t, sum_t, cross, label = [stats[:, :, member] for member in range(6)]
    best_s = jnp.max(top_s, 0)
    best_t = jnp.max(top_t, 0)
    scale_t = jnp.exp(top_t - best_t)
    total_t = jnp.sum(sum_t * scale_t, 0)
    log_student = best_s + jnp.log(jnp.sum(sum_s * jnp.exp(top_s - best_s), 0))
    losses = (
        jnp.sum(cross * scale_t, 0) / total_t
        - (best_t + jnp.log(total_t))
        + 2.0 * log_student
        - jnp.sum(label, 0)
    )
    return (block_out, embedding, losses)


def solution(mesh):
    placed = (
        P("dp", None, None, "fsdp"),
        P(None, None, "fsdp"),
        P("fsdp"),
        P(),
        P(),
        P("dp", "fsdp"),
        P("fsdp"),
        P("fsdp", "dp"),
        P("fsdp"),
        P("fsdp"),
        P("fsdp"),
        P("fsdp"),
        P("fsdp", None),
        P(("dp", "fsdp"), None),
        P(("dp", "fsdp"), None),
        P("dp", None),
        P(),
        P(),
        P(),
    )
    return jax.shard_map(
        on_device,
        mesh=mesh,
        in_specs=placed,
        out_specs=(P("dp", None, None, "fsdp"), P("dp", None), P(("dp", "fsdp"))),
        check_vma=False,
    )
```

```python
import jax
import jax.numpy as jnp
from jax import lax
from jax.experimental import pallas as pl
from jax.experimental.pallas import tpu as pltpu
from jax.sharding import PartitionSpec as P

SIDE = 8
KERNEL = 7
Z_SIDE = 8
X_SIDE = 4
Y_SIDE = 4
CORES = 2
TOKEN_TILE = 128
SQRT_HALF = 0.5**0.5
X_GROUPS = [[z * X_SIDE + x for x in range(X_SIDE)] for z in range(Z_SIDE)]
Z_GROUPS = [[z * X_SIDE + x for z in range(Z_SIDE)] for x in range(X_SIDE)]


EPSILON = 1e-06
HIGHEST = lax.Precision.HIGHEST


def depthwise(incoming_feature_maps, spatial_filter_tensor, spatial_filter_offset):
    radius = KERNEL // 2
    padded = jnp.pad(
        incoming_feature_maps.astype(jnp.float32),
        ((0, 0), (radius, radius), (radius, radius), (0, 0)),
    )
    summed = jnp.zeros(incoming_feature_maps.shape, jnp.float32)
    for vertical in range(KERNEL):
        for horizontal in range(KERNEL):
            window = padded[:, vertical : vertical + SIDE, horizontal : horizontal + SIDE, :]
            summed = (
                summed + spatial_filter_tensor[vertical, horizontal].astype(jnp.float32) * window
            )
    return (summed + spatial_filter_offset).astype(jnp.bfloat16)


def unit_rows(values):
    return (values / jnp.sqrt(jnp.sum(values * values, -1, keepdims=True) + EPSILON)).astype(
        jnp.bfloat16
    )


def logits(queries, keys, divisor):
    return (
        lax.dot_general(
            queries, keys, (((1,), (1,)), ((), ())), preferred_element_type=jnp.float32
        )
        / divisor
    )


def broadcast_gather(value, axis):
    copies = jnp.broadcast_to(value[None], (lax.axis_size(axis),) + value.shape)
    return lax.all_to_all(copies, axis, 0, 0)


def split_product(values, weights):
    top = lax.reduce_precision(values, 8, 7)
    rest = values - top
    middle = lax.reduce_precision(rest, 8, 7)
    pieces = jnp.concatenate([top, middle, rest - middle], 0).astype(jnp.bfloat16)
    product = jnp.dot(pieces, weights, preferred_element_type=jnp.float32)
    rows = values.shape[0]
    return product[2 * rows :] + product[rows : 2 * rows] + product[:rows]


def ring_pairs(size, inner, step):
    block = size // inner
    return [
        (outer * inner + place, (outer + step) % block * inner + place)
        for outer in range(block)
        for place in range(inner)
    ]


def inner_pairs(size, inner, step):
    return [
        (outer * inner + place, outer * inner + (place + step) % inner)
        for outer in range(size // inner)
        for place in range(inner)
    ]


def send_z(value, step):
    return lax.ppermute(value, "dp", ring_pairs(Z_SIDE * X_SIDE, X_SIDE, step))


def send_x(value, step):
    return lax.ppermute(value, "dp", inner_pairs(Z_SIDE * X_SIDE, X_SIDE, step))


def send_y(value, step):
    return lax.ppermute(value, "fsdp", ring_pairs(Y_SIDE * CORES, CORES, step))


def swap_cores(value):
    return lax.ppermute(value, "fsdp", inner_pairs(Y_SIDE * CORES, CORES, 1))


def both_ways(value, send):
    return send(value, 1), send(value, -1)


def both_halves(before, after, send):
    half = before.shape[0] // 2
    return send(before[:half], 1), send(after[half:], -1)


def fence(*values):
    return lax.optimization_barrier(values)


def second_kernel(preact_ref, part_ref, low_ref, high_ref, *rest):
    sources = rest[: 2 * X_SIDE]
    kept_ref, sent_ref, last, blocks, flipped, arrived = rest[2 * X_SIDE :]
    core = lax.axis_index("fsdp") % CORES
    depth = low_ref.shape[0]
    tokens = preact_ref.shape[0]
    rows = blocks.shape[1]
    members = Z_SIDE // 2
    halves = [
        pltpu.make_async_copy(
            source, last.at[pl.ds(place * depth, depth)], arrived.at[len(sources) + place]
        )
        for place, source in enumerate((low_ref, high_ref))
    ]
    copies = [
        pltpu.make_async_copy(source, blocks.at[place], arrived.at[place])
        for place, source in enumerate(sources)
    ]
    for copy in halves + copies:
        copy.start()
    for copy in halves:
        copy.wait()
    for start in range(0, tokens, TOKEN_TILE):
        tile = pl.ds(start, TOKEN_TILE)
        preact = preact_ref[tile, :] + jnp.dot(
            part_ref[tile, :], last[...], preferred_element_type=jnp.float32
        )
        hidden = preact * (1.0 + lax.erf(preact * SQRT_HALF)) * 0.5
        flipped[:, tile] = hidden.astype(jnp.bfloat16).T
    for place, copy in enumerate(copies):
        copy.wait()
        product = jnp.dot(blocks[place], flipped[...], preferred_element_type=jnp.float32)
        product = product.reshape(members, rows // members, -1)
        for pair in range(members // CORES):
            y = place % 2 * (members // CORES) + pair
            first, second = product[CORES * pair], product[CORES * pair + 1]
            kept_ref[y, place // 2] = jnp.where(core == 0, first, second).astype(jnp.bfloat16)
            sent_ref[y, place // 2] = jnp.where(core == 0, second, first).astype(jnp.bfloat16)


def second_products(preact, part, low, high, *blocks):
    tokens, depth = preact.shape
    rows = blocks[0].shape[0]
    shape = jax.ShapeDtypeStruct(
        (Y_SIDE, X_SIDE, 2 * rows // Z_SIDE, tokens), jnp.bfloat16
    )
    whole = pl.BlockSpec(memory_space=pltpu.VMEM)
    apart = pl.BlockSpec(memory_space=pl.ANY)
    kept, sent = pl.pallas_call(
        second_kernel,
        out_shape=(shape, shape),
        in_specs=[whole] * 2 + [apart] * (2 + len(blocks)),
        out_specs=(whole, whole),
        scratch_shapes=[
            pltpu.VMEM((2 * low.shape[0], depth), jnp.bfloat16),
            pltpu.VMEM((8, rows, depth), jnp.bfloat16),
            pltpu.VMEM((depth, tokens), jnp.bfloat16),
            pltpu.SemaphoreType.DMA((10,)),
        ],
        compiler_params=pltpu.CompilerParams(vmem_limit_bytes=44 * 1024 * 1024),
        cost_estimate=pl.CostEstimate(
            flops=16 * rows * depth * tokens, bytes_accessed=20 * rows * depth, transcendentals=0
        ),
    )(preact, part, low, high, *blocks)
    shape = (Y_SIDE, -1, tokens)
    return kept.reshape(shape), sent.reshape(shape)


def scatter_sums(kept, sent, y_index):
    received = swap_cores(sent)

    def both(step):
        place = (y_index + step) % Y_SIDE
        mine = lax.dynamic_index_in_dim(kept, place, 0, keepdims=False).astype(jnp.float32)
        return mine + lax.dynamic_index_in_dim(received, place, 0, keepdims=False)

    half = kept.shape[1] // 2
    far = both(2).astype(jnp.bfloat16)
    from_below = send_y(far[:half], 1)
    from_above = send_y(far[half:], -1)
    following = both(1)
    following = jnp.concatenate([following[:half] + from_below, following[half:]], 0)
    previous = both(3)
    previous = jnp.concatenate([previous[:half], previous[half:] + from_above], 0)
    below = send_y(following.astype(jnp.bfloat16), 1)
    above = send_y(previous.astype(jnp.bfloat16), -1)
    return both(0) + below + above


def on_device(
    incoming_feature_maps,
    spatial_filter_tensor,
    spatial_filter_offset,
    unit_layernorm_multiplier,
    unit_layernorm_offset_vector,
    expansion_linear_map,
    expansion_offset,
    contraction_linear_map,
    contraction_offset,
    residual_channel_factor,
    readout_layernorm_multiplier,
    readout_layernorm_offset,
    readout_linear_map,
    learner_caption_vectors,
    mentor_caption_vectors,
    mentor_picture_vectors,
    divisor_per_slot,
    active_program_slot,
    matching_caption_slot,
):
    group_count = incoming_feature_maps.shape[0]
    local_width = incoming_feature_maps.shape[3]
    shard_count = lax.axis_size("fsdp")
    shard_index = lax.axis_index("fsdp")
    data_index = lax.axis_index("dp")
    z_index = data_index // X_SIDE
    x_index = data_index % X_SIDE
    y_index = shard_index // CORES
    full_width = local_width * shard_count
    token_rows = group_count * SIDE * SIDE
    key_count = learner_caption_vectors.shape[0]
    second_rows = contraction_linear_map.shape[1]
    logit_divisor = lax.dynamic_index_in_dim(
        divisor_per_slot, active_program_slot[0], keepdims=False
    )

    own_x = lax.all_gather(
        contraction_linear_map.T, "dp", axis=0, tiled=True, axis_index_groups=Z_GROUPS
    )
    around = [send_x(expansion_linear_map, step) for step in (-1, 2, 1)]
    convolved = depthwise(incoming_feature_maps, spatial_filter_tensor, spatial_filter_offset)
    values = convolved.astype(jnp.float32).reshape(token_rows, local_width)
    sums = jnp.stack([jnp.sum(values, 1), jnp.sum(values * values, 1)])
    around, convolved, sums = fence(around, convolved, sums)

    def placed(buffer, part, step):
        return lax.dynamic_update_index_in_dim(buffer, part, (x_index + step) % X_SIDE, 0)

    block = jnp.zeros((X_SIDE,) + expansion_linear_map.shape, jnp.bfloat16)
    for step, part in enumerate([expansion_linear_map] + around):
        block = placed(block, part, step)
    first = {0: block.reshape(-1, block.shape[2])}
    first[7], first[1] = both_ways(first[0], send_z)
    totals, squares = jnp.sum(broadcast_gather(sums, "fsdp"), 0)
    mean_val = totals / full_width
    spread = squares / full_width - mean_val * mean_val
    gain_part = lax.dynamic_slice_in_dim(
        unit_layernorm_multiplier, shard_index * local_width, local_width
    )
    shift_part = lax.dynamic_slice_in_dim(
        unit_layernorm_offset_vector, shard_index * local_width, local_width
    )
    values = convolved.astype(jnp.float32).reshape(token_rows, local_width)
    local_normed = (
        (values - mean_val[:, None]) / jnp.sqrt(spread[:, None] + EPSILON) * gain_part + shift_part
    ).astype(jnp.bfloat16)
    head_rows = jnp.stack([readout_layernorm_multiplier, readout_layernorm_offset])
    head_rows = split_product(head_rows, readout_linear_map)
    teacher_rows = unit_rows(mentor_picture_vectors.astype(jnp.float32))
    own_keys = jnp.concatenate(
        [
            unit_rows(keys.astype(jnp.float32))
            for keys in (learner_caption_vectors, mentor_caption_vectors)
        ],
        1,
    )
    part_rows = own_x.shape[0] // 2
    own_low, own_high = own_x[:part_rows], own_x[part_rows:]
    first, head_rows, teacher_rows, own_keys, local_normed, own_low, own_high = fence(
        first, head_rows, teacher_rows, own_keys, local_normed, own_low, own_high
    )

    near_low = both_ways(own_low, send_x)
    first[6], first[2] = send_z(first[7], 1), send_z(first[1], -1)
    normed = lax.all_gather(local_normed, "fsdp", axis=0)
    first, near_low, own_keys = fence(first, near_low, own_keys)

    near_high = both_ways(own_high, send_x)
    far_low = send_x(near_low[0], 1)
    first[5], first[3] = send_z(first[6], 1), send_z(first[2], -1)
    all_keys = lax.all_gather(own_keys, "dp", axis=0, tiled=True)

    def part_of(place):
        return lax.dynamic_index_in_dim(normed, (z_index + place) % Z_SIDE, 0, keepdims=False)

    def first_product(place):
        return jnp.dot(part_of(place), first[place], preferred_element_type=jnp.float32)

    preact = first_product(0) + expansion_offset
    for place in (1, 7, 2, 6):
        preact = preact + first_product(place)
    first, near_high, preact = fence(first, near_high, preact)

    far_high = send_x(near_high[1], -1)
    step = both_halves(first[5], first[3], send_z)
    for place in (3, 5):
        preact = preact + first_product(place)
    last_part = part_of(4)
    step, preact, far_low, far_high, last_part = fence(step, preact, far_low, far_high, last_part)
    blocks = (own_low, own_high, near_low[1], near_high[1], far_low, far_high)
    kept, sent = second_products(preact, last_part, *step, *blocks, near_low[0], near_high[0])
    branch = scatter_sums(kept, sent, y_index)
    branch = jnp.roll(branch.reshape(X_SIDE, second_rows, token_rows), x_index, 0)
    branch = branch.reshape(local_width, token_rows).T
    residual = incoming_feature_maps.astype(jnp.float32).reshape(token_rows, local_width)
    block_out = (
        (residual + residual_channel_factor * (branch + contraction_offset))
        .astype(jnp.bfloat16)
        .reshape(incoming_feature_maps.shape)
    )
    pooled = jnp.mean(
        block_out.astype(jnp.float32).reshape(group_count, SIDE * SIDE, local_width), 1
    )
    local_mean = jnp.mean(pooled, 1, keepdims=True)
    centered = pooled - local_mean
    local_square = jnp.sum(centered * centered, 1, keepdims=True)
    product = split_product(centered * readout_layernorm_multiplier, readout_linear_map)
    local_stats = jnp.concatenate([local_mean, local_square], 1).reshape(1, -1)
    local_stats = jnp.pad(local_stats, ((0, 0), (0, product.shape[1] - local_stats.shape[1])))
    shares = broadcast_gather(jnp.concatenate([product, head_rows, local_stats], 0), "fsdp")
    head_stats = shares[:, group_count + 2, : 2 * group_count].reshape(shard_count, group_count, 2)
    means, head_squares = head_stats[:, :, 0], head_stats[:, :, 1]
    mean_val = jnp.mean(means, 0)
    offsets = means - mean_val
    spread = jnp.sum(head_squares + local_width * (offsets * offsets), 0) / full_width
    scaled = jnp.sum(
        shares[:, :group_count] + offsets[:, :, None] * shares[:, group_count, None, :], 0
    )
    embedding = scaled / jnp.sqrt(spread[:, None] + EPSILON) + jnp.sum(shares[:, group_count + 1], 0)
    student_rows = unit_rows(embedding)
    width = student_rows.shape[1]
    teacher = logits(teacher_rows, all_keys[:, teacher_rows.shape[1] :], logit_divisor)
    top_teacher = jnp.max(teacher, 1, keepdims=True)
    teacher_weights = jnp.exp(teacher - top_teacher)
    sum_teacher = jnp.sum(teacher_weights, 1)
    student = logits(student_rows, all_keys[:, :width], logit_divisor)
    local_columns = lax.iota(jnp.int32, student.shape[1])
    column_ids = (
        local_columns // key_count * shard_count + shard_index
    ) * key_count + local_columns % key_count
    labels = lax.dynamic_slice_in_dim(matching_caption_slot, data_index * group_count, group_count)
    top_student = jnp.max(student, 1, keepdims=True)
    sum_student = jnp.sum(jnp.exp(student - top_student), 1)
    label_score = jnp.sum(jnp.where(labels[:, None] == column_ids[None, :], student, 0.0), 1)
    cross_sum = jnp.sum(teacher_weights * (teacher - student), 1)
    stats = jnp.stack(
        [top_student[:, 0], sum_student, top_teacher[:, 0], sum_teacher, cross_sum, label_score], 1
    )
    per_device = group_count // shard_count
    stats = lax.all_to_all(stats.reshape(shard_count, per_device, 6), "fsdp", 0, 0)
    top_s, sum_s, top_t, sum_t, cross, label = [stats[:, :, member] for member in range(6)]
    best_s = jnp.max(top_s, 0)
    best_t = jnp.max(top_t, 0)
    scale_t = jnp.exp(top_t - best_t)
    total_t = jnp.sum(sum_t * scale_t, 0)
    log_student = best_s + jnp.log(jnp.sum(sum_s * jnp.exp(top_s - best_s), 0))
    losses = (
        jnp.sum(cross * scale_t, 0) / total_t
        - (best_t + jnp.log(total_t))
        + 2.0 * log_student
        - jnp.sum(label, 0)
    )
    return (block_out, embedding, losses)


def solution(mesh):
    placed = (
        P("dp", None, None, "fsdp"),
        P(None, None, "fsdp"),
        P("fsdp"),
        P(),
        P(),
        P("dp", "fsdp"),
        P("fsdp"),
        P("fsdp", "dp"),
        P("fsdp"),
        P("fsdp"),
        P("fsdp"),
        P("fsdp"),
        P("fsdp", None),
        P(("dp", "fsdp"), None),
        P(("dp", "fsdp"), None),
        P("dp", None),
        P(),
        P(),
        P(),
    )
    return jax.shard_map(
        on_device,
        mesh=mesh,
        in_specs=placed,
        out_specs=(P("dp", None, None, "fsdp"), P("dp", None), P(("dp", "fsdp"))),
        check_vma=False,
    )
```
